32 devices in a mesh: depth: 8 (over z, x), tok: 4 (over y, core).
Axes of the slice: x: 2, y: 2, z: 4, core: 2. Of those that a mesh axis runs over, the one named last changes fastest.
Arguments:
- states: bfloat16 [8, 4096, 2048], P('depth', 'tok'), may hold values from -40 to 40
- w_query: bfloat16 [2048, 1024], replicated, may hold values from -0.25 to 0.25
- w_key: bfloat16 [2048, 256], replicated, may hold values from -0.25 to 0.25
- w_value: bfloat16 [2048, 256], replicated, may hold values from -0.125 to 0.125
Outputs:
- window_out: bfloat16 [8, 4096, 1024], P('depth', 'tok')
- depth_out: bfloat16 [4096, 1024], P(('tok', 'depth'))
The draws below stay inside these ranges and needn't reach their ends.
All inputs are finite; a program needn't handle non-finite values.
Results may differ from the reference program's by a relative error of at most 0.012.
The reference program's roundings to bfloat16 on the way count: a program that leaves them out, or rounds other values in their place, can miss the bound.
Values may be sent and summed in bfloat16 or wider, within the bound.
No kernel may reach another device: no remote copies, remote signals or barrier semaphores. Data moves between devices by JAX's collectives and lax.ppermute only.
A program may use at most 192 MiB of HBM per device.

```python
import jax
import jax.numpy as jnp
from jax import lax

D = 2048
HQ = 8
HK = 2
HD = 128
WINDOW = 256
TOK_DEV = 1024
STEPS = 8
QW = 1024
KW = 256
TOKENS = 4096


def make_weights(key):
    base = jax.random.fold_in(key, 11)
    w_first = jax.random.normal(jax.random.fold_in(base, 1), (D, QW), jnp.float32) * D ** (-0.5)
    noise = jax.random.normal(jax.random.fold_in(base, 2), (D, KW), jnp.float32) * D ** (-0.5)
    w_second = noise
    return (jnp.clip(w_first, -0.25, 0.25), jnp.clip(w_second, -0.25, 0.25))


def draw_w_query(key, part):
    return make_weights(key)[0].astype(jnp.bfloat16)


def draw_w_key(key, part):
    return make_weights(key)[1].astype(jnp.bfloat16)


def draw_states(key, part):
    base = jax.random.fold_in(key, 23)
    noise = jax.random.normal(jax.random.fold_in(base, 1), (STEPS, TOKENS, D), jnp.float32)
    return jnp.clip(noise, -6.0, 6.0).astype(jnp.bfloat16)


def scatter_about(own_key, extent, deviation, most, kind=jnp.bfloat16):
    drawn = jax.random.normal(own_key, extent, jnp.float32) * deviation
    return jnp.minimum(jnp.maximum(drawn, -most), most).astype(kind)


def setup_inputs(seed: int = 0) -> dict:
    splits = jax.random.split(jax.random.key(seed), 5)
    states = draw_states(jax.random.fold_in(splits[4], 71), 0)
    w_query = draw_w_query(jax.random.fold_in(splits[4], 71), 0)
    w_key = draw_w_key(jax.random.fold_in(splits[4], 71), 0)
    w_value = scatter_about(splits[3], (D, KW), D ** -0.5, 0.125)
    return dict(states=states, w_query=w_query, w_key=w_key, w_value=w_value)


def project(rows, weight):
    return jnp.dot(rows, weight, preferred_element_type=jnp.float32).astype(jnp.bfloat16)

def band_block(q_block, k_block, v_block, base):
    group = HQ // HK
    q_heads = q_block.reshape(TOK_DEV, HK, group, HD).astype(jnp.float32)
    k_heads = k_block.reshape(TOK_DEV + WINDOW, HK, HD).astype(jnp.float32)
    v_heads = v_block.reshape(TOK_DEV + WINDOW, HK, HD).astype(jnp.float32)
    scores = jnp.einsum('qkgd,lkd->kgql', q_heads, k_heads) / jnp.sqrt(jnp.float32(HD))
    qpos = jnp.arange(TOK_DEV, dtype=jnp.int32)[:, None]
    kidx = jnp.arange(TOK_DEV + WINDOW, dtype=jnp.int32)[None, :]
    allowed = (kidx >= qpos) & (kidx <= qpos + WINDOW) & (base - WINDOW + kidx >= 0)
    scores = jnp.where(allowed, scores, -jnp.inf)
    top = lax.optimization_barrier(jnp.max(scores, axis=-1, keepdims=True))
    expo = jnp.exp(scores - top)
    weight = (expo / lax.optimization_barrier(jnp.sum(expo, axis=-1, keepdims=True))).astype(jnp.bfloat16)
    out = jnp.einsum('kgql,lkd->qkgd', weight.astype(jnp.float32), v_heads)
    return out.astype(jnp.bfloat16).reshape(TOK_DEV, QW)

def band_step(q_all, k_all, v_all):
    pad = jnp.zeros((WINDOW, KW), jnp.bfloat16)
    k_pad = jnp.concatenate([pad, k_all], axis=0)
    v_pad = jnp.concatenate([pad, v_all], axis=0)

    def one_block(index):
        base = index * TOK_DEV
        q_block = lax.dynamic_slice_in_dim(q_all, base, TOK_DEV, 0)
        k_block = lax.dynamic_slice_in_dim(k_pad, base, TOK_DEV + WINDOW, 0)
        v_block = lax.dynamic_slice_in_dim(v_pad, base, TOK_DEV + WINDOW, 0)
        return band_block(q_block, k_block, v_block, base)
    blocks = lax.map(one_block, jnp.arange(TOKENS // TOK_DEV, dtype=jnp.int32))
    return blocks.reshape(TOKENS, QW)

def reference(states, w_query, w_key, w_value):

    def per_step(rows):
        return (project(rows, w_query), project(rows, w_key), project(rows, w_value))
    query, key, value = lax.map(per_step, states)
    window_out = lax.map(lambda item: band_step(item[0], item[1], item[2]), (query, key, value))
    group = HQ // HK
    final_q = query[STEPS - 1].reshape(TOKENS, HK, group, HD).astype(jnp.float32)
    k_steps = key.reshape(STEPS, TOKENS, HK, HD).astype(jnp.float32)
    v_steps = value.reshape(STEPS, TOKENS, HK, HD).astype(jnp.float32)
    scores = jnp.einsum('tkgd,stkd->tkgs', final_q, k_steps) / jnp.sqrt(jnp.float32(HD))
    top = lax.optimization_barrier(jnp.max(scores, axis=-1, keepdims=True))
    expo = jnp.exp(scores - top)
    weight = expo / lax.optimization_barrier(jnp.sum(expo, axis=-1, keepdims=True))
    depth_out = jnp.einsum('tkgs,stkd->tkgd', weight, v_steps).astype(jnp.bfloat16).reshape(TOKENS, QW)
    return (window_out, depth_out)
```

```python
import functools
import math

import jax
import jax.numpy as jnp
from jax import lax
from jax.experimental import pallas as pl
from jax.experimental.pallas import tpu as pltpu
from jax.sharding import PartitionSpec as P

HQ = 8
HK = 2
HD = 128
WINDOW = 256
GROUP = HQ // HK
SCALE = 1.0 / math.sqrt(HD)
VMEM_BYTES = 48 * 1024 * 1024


def params(*semantics):
    return pltpu.CompilerParams(
        dimension_semantics=semantics or None, vmem_limit_bytes=VMEM_BYTES
    )


def project_q_kernel(x_ref, w_ref, *out_refs):
    part = out_refs[0].shape[0]
    for index, out_ref in enumerate(out_refs):
        out_ref[...] = jnp.dot(
            x_ref[pl.ds(index * part, part), :],
            w_ref[...],
            preferred_element_type=jnp.float32,
        ).astype(jnp.bfloat16)


def project_q(rows, weight, parts):
    count, depth = rows.shape
    width = weight.shape[1]
    part = count // parts
    return pl.pallas_call(
        project_q_kernel,
        out_shape=[jax.ShapeDtypeStruct((part, width), jnp.bfloat16)] * parts,
        in_specs=[pl.BlockSpec(memory_space=pltpu.VMEM)] * 2,
        out_specs=[pl.BlockSpec(memory_space=pltpu.VMEM)] * parts,
        compiler_params=params(),
        cost_estimate=pl.CostEstimate(
            flops=2 * count * depth * width,
            bytes_accessed=2 * (count * depth + depth * width + count * width),
            transcendentals=0,
        ),
    )(rows, weight)


def project_kv_kernel(x_ref, wk_ref, wv_ref, out_ref):
    width = wk_ref.shape[1]
    x = x_ref[...]
    out_ref[:, :width] = jnp.dot(x, wk_ref[...], preferred_element_type=jnp.float32).astype(jnp.bfloat16)
    out_ref[:, width:] = jnp.dot(x, wv_ref[...], preferred_element_type=jnp.float32).astype(jnp.bfloat16)


def project_kv(rows, w_key, w_value):
    count, depth = rows.shape
    width = w_key.shape[1]
    block = min(count, 256)
    whole = pl.BlockSpec((depth, width), lambda i: (0, 0))
    return pl.pallas_call(
        project_kv_kernel,
        grid=(count // block,),
        out_shape=jax.ShapeDtypeStruct((count, 2 * width), jnp.bfloat16),
        in_specs=[pl.BlockSpec((block, depth), lambda i: (i, 0)), whole, whole],
        out_specs=pl.BlockSpec((block, 2 * width), lambda i: (i, 0)),
        compiler_params=params("arbitrary"),
        cost_estimate=pl.CostEstimate(
            flops=4 * count * depth * width,
            bytes_accessed=2 * (count * depth + 2 * depth * width + 2 * count * width),
            transcendentals=0,
        ),
    )(rows, w_key, w_value)


BAND = 128


def band_kernel(parts, first_ref, *refs):
    q_refs, (kv_ref, rim_ref, out_ref) = refs[:parts], refs[parts:]
    part = q_refs[0].shape[0]
    count, width = kv_ref.shape
    width //= 2
    first = first_ref[0] == 1
    row = lax.broadcasted_iota(jnp.int32, (GROUP * BAND, BAND), 0) % BAND
    column = lax.broadcasted_iota(jnp.int32, (GROUP * BAND, BAND), 1)
    behind = column >= row
    ahead = column <= row
    ones = jnp.ones((BAND, HD), jnp.bfloat16)

    def chunk(index, low, high):
        if index < 0:
            return rim_ref[pl.ds(WINDOW + index * BAND, BAND), low:high]
        return kv_ref[pl.ds(index * BAND, BAND), low:high]

    def queries(index, head):
        start = index * BAND
        pieces = []
        size = min(part, BAND)
        for at in range(start, start + BAND, size):
            pieces.append(q_refs[at // part][pl.ds(at % part, size), head * HD : (head + 1) * HD])
        return pieces

    blocks = WINDOW // BAND + 1
    for index in range(count // BAND):
        for c in range(HK):
            q = jnp.concatenate(
                [piece for h in range(c * GROUP, (c + 1) * GROUP) for piece in queries(index, h)], axis=0
            )
            at = [index + j - (blocks - 1) for j in range(blocks)]
            k = jnp.concatenate([chunk(a, c * HD, (c + 1) * HD) for a in at], axis=0)
            v = jnp.concatenate([chunk(a, width + c * HD, width + (c + 1) * HD) for a in at], axis=0)
            v = jnp.concatenate([v, jnp.concatenate([ones] * blocks, axis=0)], axis=1)
            s = lax.dot_general(q, k, (((1,), (1,)), ((), ())), preferred_element_type=jnp.float32)
            tiles = []
            for j in range(blocks):
                t = s[:, j * BAND : (j + 1) * BAND]
                allowed = None
                if j == 0:
                    allowed = behind
                elif j == blocks - 1:
                    allowed = ahead
                if at[j] < 0:
                    some = jnp.logical_not(first)
                    allowed = some if allowed is None else jnp.logical_and(allowed, some)
                if allowed is not None:
                    t = jnp.where(allowed, t, -jnp.inf)
                tiles.append(t)
            top = functools.reduce(jnp.maximum, tiles)
            top = jnp.max(top, axis=-1, keepdims=True)
            p = jnp.concatenate(
                [jnp.exp2((t - top) * (SCALE * math.log2(math.e))).astype(jnp.bfloat16) for t in tiles], axis=1
            )
            o = jnp.dot(p, v, preferred_element_type=jnp.float32)
            o = (o[:, :HD] / o[:, HD:]).astype(jnp.bfloat16)
            for g in range(GROUP):
                h = c * GROUP + g
                out_ref[pl.ds(index * BAND, BAND), h * HD : (h + 1) * HD] = o[g * BAND : (g + 1) * BAND]


def band_attend(queries, kv, rim, first):
    parts = len(queries)
    count = kv.shape[0]
    width = queries[0].shape[1]
    vmem = pl.BlockSpec(memory_space=pltpu.VMEM)
    return pl.pallas_call(
        functools.partial(band_kernel, parts),
        out_shape=jax.ShapeDtypeStruct((count, width), jnp.bfloat16),
        in_specs=[pl.BlockSpec(memory_space=pltpu.SMEM)] + [vmem] * (parts + 2),
        out_specs=vmem,
        compiler_params=params(),
        cost_estimate=pl.CostEstimate(
            flops=4 * count * width * (WINDOW + BAND),
            bytes_accessed=4 * count * width + 2 * kv.size,
            transcendentals=HQ * count * (WINDOW + BAND),
        ),
    )(first, *queries, kv, rim)


def depth_kernel(q_ref, kv_ref, out_ref):
    steps, count, width = kv_ref.shape
    width //= 2
    chunk = min(count, 32)
    for start in range(0, count, chunk):
        rows = pl.ds(start, chunk)
        for c in range(HK):
            keys = [kv_ref[s, rows, c * HD : (c + 1) * HD].astype(jnp.float32) for s in range(steps)]
            values = [
                kv_ref[s, rows, width + c * HD : width + (c + 1) * HD].astype(jnp.float32) for s in range(steps)
            ]
            for h in range(c * GROUP, (c + 1) * GROUP):
                q = q_ref[rows, h * HD : (h + 1) * HD].astype(jnp.float32)
                scores = [jnp.sum(q * k, axis=-1, keepdims=True) * SCALE for k in keys]
                top = functools.reduce(jnp.maximum, scores)
                expo = [jnp.exp(s - top) for s in scores]
                total = functools.reduce(jnp.add, expo)
                out = functools.reduce(jnp.add, [e * v for e, v in zip(expo, values)])
                out_ref[rows, h * HD : (h + 1) * HD] = (out / total).astype(jnp.bfloat16)


def depth_attend(query, kv):
    vmem = pl.BlockSpec(memory_space=pltpu.VMEM)
    return pl.pallas_call(
        depth_kernel,
        out_shape=jax.ShapeDtypeStruct(query.shape, jnp.bfloat16),
        in_specs=[vmem] * 2,
        out_specs=vmem,
        compiler_params=params(),
        cost_estimate=pl.CostEstimate(
            flops=4 * query.size * kv.shape[0],
            bytes_accessed=2 * (2 * query.size + kv.size),
            transcendentals=query.shape[0] * HQ * kv.shape[0],
        ),
    )(query, kv)


def scatter_last(blocks, axis):
    count = len(blocks)
    here = lax.axis_index(axis)
    mine = blocks[count - 1]
    for index in range(count - 1):
        got = lax.ppermute(blocks[index], axis, [(count - 1, index)])
        mine = jnp.where(here == index, got, mine)
    return mine


def body(states, w_query, w_key, w_value):
    local = states[0]
    rows = local.shape[0]
    steps = lax.axis_size("depth")
    part = rows // steps
    shards = lax.axis_size("tok")
    queries = project_q(local, w_query, steps)
    kv = project_kv(local, w_key, w_value)
    rim = lax.ppermute(kv[rows - WINDOW :], "tok", [(t, t + 1) for t in range(shards - 1)])
    spread = lax.all_to_all(kv.reshape(steps, part, kv.shape[1]), "depth", split_axis=0, concat_axis=0, tiled=True)
    first = (lax.axis_index("tok") == 0).astype(jnp.int32).reshape(1)
    window_out = band_attend(queries, kv, rim, first)
    final_q = scatter_last(queries, "depth")
    depth_out = depth_attend(final_q, spread)
    return (window_out[None], depth_out)


def solution(mesh):
    in_specs = (P("depth", "tok", None), P(), P(), P())
    out_specs = (P("depth", "tok", None), P(("tok", "depth"), None))
    return jax.shard_map(body, mesh=mesh, in_specs=in_specs, out_specs=out_specs, check_vma=False)
```

```python
import functools
import math

import jax
import jax.numpy as jnp
from jax import lax
from jax.experimental import pallas as pl
from jax.experimental.pallas import tpu as pltpu
from jax.sharding import PartitionSpec as P

HQ = 8
HK = 2
HD = 128
WINDOW = 256
GROUP = HQ // HK
SCALE = 1.0 / math.sqrt(HD)
BAND = 128
RELAYS = 2
LAST_FLOPS = 10**9
MIB = 1024 * 1024
VMEM = pl.BlockSpec(memory_space=pltpu.VMEM)
SMEM = pl.BlockSpec(memory_space=pltpu.SMEM)
ANY = pl.BlockSpec(memory_space=pl.ANY)
HBM = pl.BlockSpec(memory_space=pltpu.HBM)


def params(mib):
    return pltpu.CompilerParams(vmem_limit_bytes=mib * MIB)


def array(*shape):
    return jax.ShapeDtypeStruct(shape, jnp.bfloat16)


def buffer(*shape):
    return pltpu.VMEM(shape, jnp.bfloat16)


def hbm_array(*shape):
    return pltpu.HBM(shape, jnp.bfloat16)


def in_hbm(*arrays):
    return [pltpu.with_memory_space_constraint(a, pltpu.HBM) for a in arrays]


def cost(flops=1):
    return pl.CostEstimate(flops=flops, bytes_accessed=1, transcendentals=0)


def matmul(x, w):
    return jnp.dot(x, w, preferred_element_type=jnp.float32).astype(jnp.bfloat16)


def project_kv_kernel(x_hbm, wk_hbm, wv_hbm, kv_hbm, rim_hbm, kv_ref, x_ref, wk_ref, wv_ref, in_sems, out_sems):
    chunks, size = x_ref.shape[:2]
    width = wk_ref.shape[1]
    slices = [pl.ds(i * size, size) for i in range(chunks)]
    load_k = pltpu.make_async_copy(wk_hbm, wk_ref, in_sems.at[0])
    load_v = pltpu.make_async_copy(wv_hbm, wv_ref, in_sems.at[1])
    load_x = [
        pltpu.make_async_copy(x_hbm.at[at], x_ref.at[i], in_sems.at[2 + i]) for i, at in enumerate(slices)
    ]
    load_k.start()
    load_x[0].start()
    load_v.start()
    for load in load_x[1:]:
        load.start()
    load_k.wait()
    stores = []
    for i, at in enumerate(slices):
        load_x[i].wait()
        kv_ref[at, :width] = matmul(x_ref[i], wk_ref[...])
        if not i:
            load_v.wait()
        kv_ref[at, width:] = matmul(x_ref[i], wv_ref[...])
        stores.append(pltpu.make_async_copy(kv_ref.at[at], kv_hbm.at[at], out_sems.at[i]))
        stores[-1].start()
    last = pl.ds(chunks * size - WINDOW, WINDOW)
    stores.append(pltpu.make_async_copy(kv_ref.at[last], rim_hbm, out_sems.at[chunks]))
    stores[-1].start()
    for store in stores:
        store.wait()


def project_kv(rows, w_key, w_value):
    count, depth = rows.shape
    width = w_key.shape[1]
    size = min(count, 256)
    chunks = count // size
    return pl.pallas_call(
        project_kv_kernel,
        out_shape=[hbm_array(count, 2 * width), hbm_array(WINDOW, 2 * width), array(count, 2 * width)],
        in_specs=[HBM] * 3,
        out_specs=[HBM] * 2 + [VMEM],
        scratch_shapes=[
            buffer(chunks, size, depth),
            buffer(depth, width),
            buffer(depth, width),
            pltpu.SemaphoreType.DMA((2 + chunks,)),
            pltpu.SemaphoreType.DMA((1 + chunks,)),
        ],
        compiler_params=params(16),
        cost_estimate=cost(),
    )(*in_hbm(rows, w_key, w_value))


def project_q_kernel(part, pick, x_hbm, w_hbm, q_ref, *refs):
    out_refs, (x_ref, w_ref, in_sems, out_sems) = refs[:-4], refs[-4:]
    chunks, size = x_ref.shape[:2]
    slices = [pl.ds(i * size, size) for i in range(chunks)]
    load_w = pltpu.make_async_copy(w_hbm, w_ref, in_sems.at[chunks])
    load_x = [pltpu.make_async_copy(x_hbm.at[at], x_ref.at[i], in_sems.at[i]) for i, at in enumerate(slices)]
    load_w.start()
    for load in load_x:
        load.start()
    load_w.wait()
    stores = []
    for i, at in enumerate(slices):
        load_x[i].wait()
        q_ref[at, :] = matmul(x_ref[i], w_ref[...])
        for number, index in enumerate(pick):
            if i * size < (index + 1) * part <= (i + 1) * size:
                source = q_ref.at[pl.ds(index * part, part)]
                stores.append(pltpu.make_async_copy(source, out_refs[number], out_sems.at[number]))
                stores[-1].start()
    for store in stores:
        store.wait()


def project_q(rows, weight, part, pick):
    count = rows.shape[0]
    depth, width = weight.shape
    size = min(count, 256)
    return pl.pallas_call(
        functools.partial(project_q_kernel, part, pick),
        out_shape=[array(count, width)] + [hbm_array(part, width)] * len(pick),
        in_specs=[HBM] * 2,
        out_specs=[VMEM] + [HBM] * len(pick),
        scratch_shapes=[
            buffer(count // size, size, depth),
            buffer(depth, width),
            pltpu.SemaphoreType.DMA((1 + count // size,)),
            pltpu.SemaphoreType.DMA((len(pick),)),
        ],
        compiler_params=params(16),
        cost_estimate=cost(),
    )(*in_hbm(rows, weight))


def choose_kernel(which_ref, a_hbm, b_hbm, *refs):
    out_ref, sem = refs[-2:]
    for flag, source in ((1, a_hbm), (0, b_hbm)):

        @pl.when(which_ref[0] == flag)
        def _(source=source):
            pltpu.make_async_copy(source, out_ref, sem).start()

    pltpu.make_async_copy(b_hbm, out_ref, sem).wait()


def choose(which, a, b, after):
    return pl.pallas_call(
        choose_kernel,
        out_shape=array(*a.shape),
        in_specs=[SMEM] + [HBM] * 2 + [ANY] * len(after),
        out_specs=VMEM,
        scratch_shapes=[pltpu.SemaphoreType.DMA],
        compiler_params=params(16),
        cost_estimate=cost(),
    )(which, *in_hbm(a, b), *after)


def band_kernel(blocks_of, first_ref, q_ref, kv_ref, *refs):
    rim_ref, (out_hbm, token_ref, out_ref, sems) = refs[0], refs[-4:]
    token_ref[...] = jnp.zeros_like(token_ref)
    width = kv_ref.shape[1] // 2
    first = first_ref[0] == 1
    row = lax.broadcasted_iota(jnp.int32, (GROUP * BAND, BAND), 0) % BAND
    column = lax.broadcasted_iota(jnp.int32, (GROUP * BAND, BAND), 1)
    behind = column >= row
    ahead = column <= row
    ones = jnp.ones((BAND, HD), jnp.bfloat16)

    def chunk(index, low, high):
        if index < 0:
            return rim_ref[pl.ds(WINDOW + index * BAND, BAND), low:high]
        return kv_ref[pl.ds(index * BAND, BAND), low:high]

    blocks = WINDOW // BAND + 1
    stores = []
    for number, index in enumerate(blocks_of):
        for c in range(HK):
            q = jnp.concatenate(
                [q_ref[pl.ds(index * BAND, BAND), h * HD : (h + 1) * HD] for h in range(c * GROUP, (c + 1) * GROUP)],
                axis=0,
            )
            at = [index + j - (blocks - 1) for j in range(blocks)]
            k = jnp.concatenate([chunk(a, c * HD, (c + 1) * HD) for a in at], axis=0)
            v = jnp.concatenate([chunk(a, width + c * HD, width + (c + 1) * HD) for a in at], axis=0)
            v = jnp.concatenate([v, jnp.concatenate([ones] * blocks, axis=0)], axis=1)
            s = lax.dot_general(q, k, (((1,), (1,)), ((), ())), preferred_element_type=jnp.float32)
            tiles = []
            for j in range(blocks):
                t = s[:, j * BAND : (j + 1) * BAND]
                allowed = None
                if j == 0:
                    allowed = behind
                elif j == blocks - 1:
                    allowed = ahead
                if at[j] < 0:
                    some = jnp.logical_not(first)
                    allowed = some if allowed is None else jnp.logical_and(allowed, some)
                if allowed is not None:
                    t = jnp.where(allowed, t, -jnp.inf)
                tiles.append(t)
            top = functools.reduce(jnp.maximum, tiles)
            top = jnp.max(top, axis=-1, keepdims=True)
            p = jnp.concatenate(
                [jnp.exp2((t - top) * (SCALE * math.log2(math.e))).astype(jnp.bfloat16) for t in tiles], axis=1
            )
            o = jnp.dot(p, v, preferred_element_type=jnp.float32)
            o = (o[:, :HD] / o[:, HD:]).astype(jnp.bfloat16)
            for g in range(GROUP):
                h = c * GROUP + g
                out_ref[pl.ds(number * BAND, BAND), h * HD : (h + 1) * HD] = o[g * BAND : (g + 1) * BAND]
        stores.append(
            pltpu.make_async_copy(
                out_ref.at[pl.ds(number * BAND, BAND)], out_hbm.at[pl.ds(index * BAND, BAND)], sems.at[number]
            )
        )
        stores[-1].start()
    for store in stores:
        store.wait()


def band_attend(first, query, kv, rim, blocks_of, out, after, flops=1):
    count, width = query.shape
    rows = len(blocks_of) * BAND
    inside = [rim] if blocks_of[0] * BAND < WINDOW else []
    given = [] if out is None else [out]
    return pl.pallas_call(
        functools.partial(band_kernel, blocks_of),
        out_shape=[array(count, width), array(16, HD)],
        in_specs=[SMEM] + [VMEM] * (2 + len(inside)) + [ANY] * len(given + after),
        out_specs=[ANY, VMEM],
        scratch_shapes=[buffer(rows, width), pltpu.SemaphoreType.DMA((len(blocks_of),))],
        input_output_aliases={3 + len(inside): 0} if given else {},
        compiler_params=params(16),
        cost_estimate=cost(flops),
    )(first, query, kv, *inside, *given, *after)


def depth_kernel(which_ref, *refs):
    q_refs, (kv_ref, out_ref, q_ref) = refs[:-3], refs[-3:]
    steps, count, width = kv_ref.shape
    width //= 2
    for case, ref in enumerate(q_refs):

        @pl.when(which_ref[0] == case)
        def _(ref=ref):
            q_ref[...] = ref[...]

    chunk = min(count, 32)
    for start in range(0, count, chunk):
        rows = pl.ds(start, chunk)
        for c in range(HK):
            keys = [kv_ref[s, rows, c * HD : (c + 1) * HD].astype(jnp.float32) for s in range(steps)]
            values = [
                kv_ref[s, rows, width + c * HD : width + (c + 1) * HD].astype(jnp.float32) for s in range(steps)
            ]
            for h in range(c * GROUP, (c + 1) * GROUP):
                q = q_ref[rows, h * HD : (h + 1) * HD].astype(jnp.float32)
                scores = [jnp.sum(q * k, axis=-1, keepdims=True) * SCALE for k in keys]
                top = functools.reduce(jnp.maximum, scores)
                expo = [jnp.exp(s - top) for s in scores]
                total = functools.reduce(jnp.add, expo)
                out = functools.reduce(jnp.add, [e * v for e, v in zip(expo, values)])
                out_ref[rows, h * HD : (h + 1) * HD] = (out / total).astype(jnp.bfloat16)


def depth_attend(which, queries, kv):
    shape = queries[0].shape
    size = queries[0].size
    return pl.pallas_call(
        depth_kernel,
        out_shape=array(*shape),
        in_specs=[SMEM] + [VMEM] * (len(queries) + 1),
        out_specs=VMEM,
        scratch_shapes=[buffer(*shape)],
        compiler_params=params(16),
        cost_estimate=cost(),
    )(which, *queries, kv)


def flag(value):
    return value.astype(jnp.int32).reshape(1)


def body(states, w_query, w_key, w_value):
    local = states[0]
    rows = local.shape[0]
    steps = lax.axis_size("depth")
    here = lax.axis_index("depth")
    part = rows // steps
    shards = lax.axis_size("tok")
    root, buddy = steps - 1, steps - 2
    first = flag(lax.axis_index("tok") == 0)
    is_root = flag(here == root)
    by_buddy = list(range(0, buddy, 2))[:RELAYS]
    straight = [i for i in range(buddy) if i // 2 * 2 not in by_buddy]

    kv, rim, own = project_kv(local, w_key, w_value)
    spread = lax.all_to_all(kv.reshape(steps, part, kv.shape[1]), "depth", split_axis=0, concat_axis=0, tiled=True)
    rim = lax.ppermute(rim, "tok", [(t, t + 1) for t in range(shards - 1)])
    query, *queries = project_q(local, w_query, part, list(range(steps)))

    relayed = [lax.ppermute(queries[index], "depth", [(root, buddy)]) for index in by_buddy]
    direct = [lax.ppermute(queries[index], "depth", [(root, index)]) for index in straight]
    owners = [(queries[root], [root])] + [(q, [index]) for q, index in zip(direct, straight)]
    blocks = list(range(rows // BAND))
    calls = len(by_buddy) + 1
    window_out, after = None, []
    for turn in range(calls):
        low, high = len(blocks) * (calls - 1 - turn) // calls, len(blocks) * (calls - turn) // calls
        flops = LAST_FLOPS if turn == calls - 1 else 1
        window_out, token = band_attend(first, query, own, rim, blocks[low:high], window_out, after, flops)
        after = []
        if turn < calls - 1:
            index = by_buddy[turn]
            last = turn == calls - 2
            block = choose(is_root, queries[index + 1], relayed[turn], [token] + (direct if last else []))
            got = lax.ppermute(block, "depth", [(buddy, index), (root, index + 1)])
            owners.append((got, [index, index + 1]))
            if last:
                after = [q for q, _ in owners[1 + len(direct) : -1]]
    owners.append((lax.ppermute(queries[buddy], "depth", [(root, buddy)]), [buddy]))
    which = sum((jnp.where(here == i, case, 0) for case, (_, found) in enumerate(owners) for i in found), 0)
    depth_out = depth_attend(flag(which), [q for q, _ in owners], spread)
    return (window_out[None], depth_out)


def solution(mesh):
    in_specs = (P("depth", "tok", None), P(), P(), P())
    out_specs = (P("depth", "tok", None), P(("tok", "depth"), None))
    return jax.shard_map(body, mesh=mesh, in_specs=in_specs, out_specs=out_specs, check_vma=False)
```

```python
import functools
import math

import jax
import jax.numpy as jnp
from jax import lax
from jax.experimental import pallas as pl
from jax.experimental.pallas import tpu as pltpu
from jax.sharding import PartitionSpec as P

HQ = 8
HK = 2
HD = 128
WINDOW = 256
GROUP = HQ // HK
SCALE = 1.0 / math.sqrt(HD)
BAND = 128
RELAYS = 2
LAST_FLOPS = 10**9
PIECES = 4
LAST_ROWS = 256
MIB = 1024 * 1024
VMEM = pl.BlockSpec(memory_space=pltpu.VMEM)
SMEM = pl.BlockSpec(memory_space=pltpu.SMEM)
ANY = pl.BlockSpec(memory_space=pl.ANY)
HBM = pl.BlockSpec(memory_space=pltpu.HBM)


def params(mib):
    return pltpu.CompilerParams(vmem_limit_bytes=mib * MIB)


def array(*shape):
    return jax.ShapeDtypeStruct(shape, jnp.bfloat16)


def buffer(*shape):
    return pltpu.VMEM(shape, jnp.bfloat16)


def hbm_array(*shape):
    return pltpu.HBM(shape, jnp.bfloat16)


def in_hbm(*arrays):
    return [pltpu.with_memory_space_constraint(a, pltpu.HBM) for a in arrays]


def cost(flops=1):
    return pl.CostEstimate(flops=flops, bytes_accessed=1, transcendentals=0)


def accumulate(loads, x_ref, w_ref, acc_ref, out_ref, store):
    pieces, count, _ = x_ref.shape
    for i in range(pieces):
        for load in loads[i]:
            load.wait()
        chunk = count if i < pieces - 1 else min(count, LAST_ROWS)
        for start in range(0, count, chunk):
            at = pl.ds(start, chunk)
            term = jnp.dot(x_ref[i, at, :], w_ref[i], preferred_element_type=jnp.float32)
            if i:
                term = acc_ref[at, :] + term
            if i < pieces - 1:
                acc_ref[at, :] = term
            else:
                out_ref[at, :] = term.astype(jnp.bfloat16)
                store(start, chunk)


def load_pieces(x_hbm, x_ref, w_hbms, w_ref, sems):
    pieces, _, size = x_ref.shape
    loads = []
    for i in range(pieces):
        at, left = pl.ds(i * size, size), 0
        loads.append([pltpu.make_async_copy(x_hbm.at[:, at], x_ref.at[i], sems.at[i, 0])])
        for number, w_hbm in enumerate(w_hbms):
            width = w_hbm.shape[1]
            target = w_ref.at[i, :, pl.ds(left, width)]
            loads[-1].append(pltpu.make_async_copy(w_hbm.at[at], target, sems.at[i, 1 + number]))
            left += width
        for load in loads[-1]:
            load.start()
    return loads


def project_kv_kernel(x_hbm, wk_hbm, wv_hbm, kv_hbm, rim_hbm, x_ref, w_ref, acc_ref, kv_ref, in_sems, out_sems):
    loads = load_pieces(x_hbm, x_ref, [wk_hbm, wv_hbm], w_ref, in_sems)
    stores = []

    def store(start, chunk):
        at = pl.ds(start, chunk)
        stores.append(pltpu.make_async_copy(kv_ref.at[at], kv_hbm.at[at], out_sems.at[len(stores)]))
        stores[-1].start()

    accumulate(loads, x_ref, w_ref, acc_ref, kv_ref, store)
    last = pl.ds(kv_ref.shape[0] - WINDOW, WINDOW)
    stores.append(pltpu.make_async_copy(kv_ref.at[last], rim_hbm, out_sems.at[len(stores)]))
    stores[-1].start()
    for copy in stores:
        copy.wait()


def project_kv(rows, w_key, w_value):
    count, depth = rows.shape
    width = w_key.shape[1]
    return pl.pallas_call(
        project_kv_kernel,
        out_shape=[hbm_array(count, 2 * width), hbm_array(WINDOW, 2 * width)],
        in_specs=[HBM] * 3,
        out_specs=[HBM] * 2,
        scratch_shapes=[
            buffer(PIECES, count, depth // PIECES),
            buffer(PIECES, depth // PIECES, 2 * width),
            pltpu.VMEM((count, 2 * width), jnp.float32),
            buffer(count, 2 * width),
            pltpu.SemaphoreType.DMA((PIECES, 3)),
            pltpu.SemaphoreType.DMA((1 + -(-count // min(count, LAST_ROWS)),)),
        ],
        compiler_params=params(16),
        cost_estimate=cost(),
    )(*in_hbm(rows, w_key, w_value))


def project_q_kernel(part, x_hbm, w_hbm, q_ref, *refs):
    part_hbms, (x_ref, w_ref, acc_ref, in_sems, out_sems) = refs[:-5], refs[-5:]
    loads = load_pieces(x_hbm, x_ref, [w_hbm], w_ref, in_sems)
    stores = []

    def store(start, chunk):
        for index in range(len(part_hbms)):
            if start < (index + 1) * part <= start + chunk:
                source = q_ref.at[pl.ds(index * part, part)]
                stores.append(pltpu.make_async_copy(source, part_hbms[index], out_sems.at[index]))
                stores[-1].start()

    accumulate(loads, x_ref, w_ref, acc_ref, q_ref, store)
    for copy in stores:
        copy.wait()


def project_q(rows, weight, parts):
    count, depth = rows.shape
    width = weight.shape[1]
    part = count // parts
    return pl.pallas_call(
        functools.partial(project_q_kernel, part),
        out_shape=[array(count, width)] + [hbm_array(part, width)] * (parts - 1),
        in_specs=[HBM] * 2,
        out_specs=[VMEM] + [HBM] * (parts - 1),
        scratch_shapes=[
            buffer(PIECES, count, depth // PIECES),
            buffer(PIECES, depth // PIECES, width),
            pltpu.VMEM((count, width), jnp.float32),
            pltpu.SemaphoreType.DMA((PIECES, 2)),
            pltpu.SemaphoreType.DMA((parts - 1,)),
        ],
        compiler_params=params(20),
        cost_estimate=cost(),
    )(*in_hbm(rows, weight))


def nothing_kernel(*refs):
    pass


def once(block, arrays):
    return pl.pallas_call(
        nothing_kernel,
        out_shape=hbm_array(*block.shape),
        in_specs=[HBM] + [ANY] * len(arrays),
        out_specs=HBM,
        input_output_aliases={0: 0},
        cost_estimate=cost(),
    )(*in_hbm(block), *arrays)


def choose_kernel(which_ref, a_hbm, b_hbm, *refs):
    out_ref, sem = refs[-2:]
    for flag, source in ((1, a_hbm), (0, b_hbm)):

        @pl.when(which_ref[0] == flag)
        def _(source=source):
            pltpu.make_async_copy(source, out_ref, sem).start()

    pltpu.make_async_copy(b_hbm, out_ref, sem).wait()


def choose(which, a, b, after):
    return pl.pallas_call(
        choose_kernel,
        out_shape=array(*a.shape),
        in_specs=[SMEM] + [HBM] * 2 + [ANY] * len(after),
        out_specs=VMEM,
        scratch_shapes=[pltpu.SemaphoreType.DMA],
        compiler_params=params(16),
        cost_estimate=cost(),
    )(which, *in_hbm(a, b), *after)


def band_kernel(blocks_of, first_ref, q_ref, kv_ref, *refs):
    rim_ref, (out_hbm, token_ref, out_ref, sems) = refs[0], refs[-4:]
    token_ref[...] = jnp.zeros_like(token_ref)
    width = kv_ref.shape[1] // 2
    first = first_ref[0] == 1
    row = lax.broadcasted_iota(jnp.int32, (GROUP * BAND, BAND), 0) % BAND
    column = lax.broadcasted_iota(jnp.int32, (GROUP * BAND, BAND), 1)
    behind = column >= row
    ahead = column <= row
    ones = jnp.ones((BAND, HD), jnp.bfloat16)

    def chunk(index, low, high):
        if index < 0:
            return rim_ref[pl.ds(WINDOW + index * BAND, BAND), low:high]
        return kv_ref[pl.ds(index * BAND, BAND), low:high]

    blocks = WINDOW // BAND + 1
    stores = []
    for number, index in enumerate(blocks_of):
        for c in range(HK):
            q = jnp.concatenate(
                [q_ref[pl.ds(index * BAND, BAND), h * HD : (h + 1) * HD] for h in range(c * GROUP, (c + 1) * GROUP)],
                axis=0,
            )
            at = [index + j - (blocks - 1) for j in range(blocks)]
            k = jnp.concatenate([chunk(a, c * HD, (c + 1) * HD) for a in at], axis=0)
            v = jnp.concatenate([chunk(a, width + c * HD, width + (c + 1) * HD) for a in at], axis=0)
            v = jnp.concatenate([v, jnp.concatenate([ones] * blocks, axis=0)], axis=1)
            s = lax.dot_general(q, k, (((1,), (1,)), ((), ())), preferred_element_type=jnp.float32)
            tiles = []
            for j in range(blocks):
                t = s[:, j * BAND : (j + 1) * BAND]
                allowed = None
                if j == 0:
                    allowed = behind
                elif j == blocks - 1:
                    allowed = ahead
                if at[j] < 0:
                    some = jnp.logical_not(first)
                    allowed = some if allowed is None else jnp.logical_and(allowed, some)
                if allowed is not None:
                    t = jnp.where(allowed, t, -jnp.inf)
                tiles.append(t)
            top = functools.reduce(jnp.maximum, tiles)
            top = jnp.max(top, axis=-1, keepdims=True)
            p = jnp.concatenate(
                [jnp.exp2((t - top) * (SCALE * math.log2(math.e))).astype(jnp.bfloat16) for t in tiles], axis=1
            )
            o = jnp.dot(p, v, preferred_element_type=jnp.float32)
            o = (o[:, :HD] / o[:, HD:]).astype(jnp.bfloat16)
            for g in range(GROUP):
                h = c * GROUP + g
                out_ref[pl.ds(number * BAND, BAND), h * HD : (h + 1) * HD] = o[g * BAND : (g + 1) * BAND]
        stores.append(
            pltpu.make_async_copy(
                out_ref.at[pl.ds(number * BAND, BAND)], out_hbm.at[pl.ds(index * BAND, BAND)], sems.at[number]
            )
        )
        stores[-1].start()
    for store in stores:
        store.wait()


def band_attend(first, query, kv, rim, blocks_of, out, after, flops=1):
    count, width = query.shape
    rows = len(blocks_of) * BAND
    inside = [rim] if blocks_of[0] * BAND < WINDOW else []
    given = [] if out is None else [out]
    return pl.pallas_call(
        functools.partial(band_kernel, blocks_of),
        out_shape=[array(count, width), array(16, HD)],
        in_specs=[SMEM] + [VMEM] * (2 + len(inside)) + [ANY] * len(given + after),
        out_specs=[ANY, VMEM],
        scratch_shapes=[buffer(rows, width), pltpu.SemaphoreType.DMA((len(blocks_of),))],
        input_output_aliases={3 + len(inside): 0} if given else {},
        compiler_params=params(16),
        cost_estimate=cost(flops),
    )(first, query, kv, *inside, *given, *after)


def depth_kernel(cases, which_ref, *refs):
    q_hbms, (kv_hbm, out_hbm, q_ref, kv_ref, out_ref, sems) = refs[:cases], refs[cases:]
    steps, count, width = kv_ref.shape
    width //= 2
    chunk = min(count, 32)
    chunks = [pl.ds(start, chunk) for start in range(0, count, chunk)]
    last = pl.ds(q_hbms[0].shape[0] - count, count)
    loads = []
    for case, source in enumerate([q_hbms[0].at[last], *q_hbms[1:]]):

        @pl.when(which_ref[0] == case)
        def _(source=source):
            pltpu.make_async_copy(source, q_ref, sems.at[0]).start()

    for i, rows in enumerate(chunks):
        loads.append(pltpu.make_async_copy(kv_hbm.at[:, rows], kv_ref.at[:, rows], sems.at[1 + i]))
        loads[-1].start()
    pltpu.make_async_copy(q_hbms[1], q_ref, sems.at[0]).wait()
    stores = []
    for i, rows in enumerate(chunks):
        loads[i].wait()
        for c in range(HK):
            keys = [kv_ref[s, rows, c * HD : (c + 1) * HD].astype(jnp.float32) for s in range(steps)]
            values = [
                kv_ref[s, rows, width + c * HD : width + (c + 1) * HD].astype(jnp.float32) for s in range(steps)
            ]
            for h in range(c * GROUP, (c + 1) * GROUP):
                q = q_ref[rows, h * HD : (h + 1) * HD].astype(jnp.float32) * (SCALE * math.log2(math.e))
                scores = [jnp.sum(q * k, axis=-1, keepdims=True) for k in keys]
                top = functools.reduce(jnp.maximum, scores)
                expo = [jnp.exp2(s - top) for s in scores]
                part = 1.0 / functools.reduce(jnp.add, expo)
                out = functools.reduce(jnp.add, [(e * part) * v for e, v in zip(expo, values)])
                out_ref[rows, h * HD : (h + 1) * HD] = out.astype(jnp.bfloat16)
        stores.append(pltpu.make_async_copy(out_ref.at[rows], out_hbm.at[rows], sems.at[1 + len(chunks) + i]))
        stores[-1].start()
    for store in stores:
        store.wait()


def depth_attend(which, query, queries, kv):
    steps, count, _ = kv.shape
    shape = (count, query.shape[1])
    return pl.pallas_call(
        functools.partial(depth_kernel, 1 + len(queries)),
        out_shape=array(*shape),
        in_specs=[SMEM, ANY] + [HBM] * len(queries) + [HBM],
        out_specs=ANY,
        scratch_shapes=[
            buffer(*shape),
            buffer(*kv.shape),
            buffer(*shape),
            pltpu.SemaphoreType.DMA((1 + 2 * -(-count // min(count, 32)),)),
        ],
        compiler_params=params(16),
        cost_estimate=cost(),
    )(which, query, *in_hbm(*queries, kv))


def flag(value):
    return value.astype(jnp.int32).reshape(1)


def body(states, w_query, w_key, w_value):
    local = states[0]
    rows = local.shape[0]
    steps = lax.axis_size("depth")
    here = lax.axis_index("depth")
    part = rows // steps
    shards = lax.axis_size("tok")
    root, buddy = steps - 1, steps - 2
    first = flag(lax.axis_index("tok") == 0)
    is_root = flag(here == root)
    by_buddy = list(range(0, buddy, 2))[-RELAYS:]
    straight = [i for i in range(buddy) if i // 2 * 2 not in by_buddy]

    def send(block, *pairs):
        return lax.ppermute(block, "depth", list(pairs))

    kv, rim = project_kv(local, w_key, w_value)
    spread = lax.all_to_all(kv.reshape(steps, part, kv.shape[1]), "depth", split_axis=0, concat_axis=0, tiled=True)
    rim = lax.ppermute(rim, "tok", [(t, (t + 1) % shards) for t in range(shards)])
    query, *queries = project_q(local, w_query, steps)

    relayed = [send(queries[index], (root, buddy)) for index in by_buddy]
    direct = [send(queries[index], (root, index)) for index in straight]
    blocks = list(range(rows // BAND))
    calls = len(by_buddy) + 1
    window_out, after, beside = None, [], []
    for turn in range(calls):
        low, high = len(blocks) * (calls - 1 - turn) // calls, len(blocks) * (calls - turn) // calls
        flops = LAST_FLOPS if turn == calls - 1 else 1
        window_out, token = band_attend(first, query, kv, rim, blocks[low:high], window_out, after, flops)
        if turn < calls - 1:
            index = by_buddy[turn]
            last = turn == calls - 2
            block = choose(is_root, queries[index + 1], relayed[turn], [token] + (direct if last else []))
            if last:
                after = list(beside)
            beside.append(send(block, (buddy, index), (root, index + 1)))
    own = send(once(queries[buddy], [block]), (root, buddy))
    owners = [[i] for i in straight] + [[i, i + 1] for i in by_buddy] + [[buddy]]
    which = sum((jnp.where(here == i, case + 1, 0) for case, ends in enumerate(owners) for i in ends), 0)
    depth_out = depth_attend(flag(which), query, direct + beside + [own], spread)
    return (window_out[None], depth_out)


def solution(mesh):
    in_specs = (P("depth", "tok", None), P(), P(), P())
    out_specs = (P("depth", "tok", None), P(("tok", "depth"), None))
    return jax.shard_map(body, mesh=mesh, in_specs=in_specs, out_specs=out_specs, check_vma=False)
```

```python
import functools
import math

import jax
import jax.numpy as jnp
from jax import lax
from jax.experimental import pallas as pl
from jax.experimental.pallas import tpu as pltpu
from jax.sharding import PartitionSpec as P

HQ = 8
HK = 2
HD = 128
WINDOW = 256
GROUP = HQ // HK
SCALE = 1.0 / math.sqrt(HD)
BAND = 128
RELAYS = 2
LAST_FLOPS = 10**9
PIECES = 4
BAND_LAST = 3
LAST_ROWS = 256
MIB = 1024 * 1024
VMEM = pl.BlockSpec(memory_space=pltpu.VMEM)
SMEM = pl.BlockSpec(memory_space=pltpu.SMEM)
ANY = pl.BlockSpec(memory_space=pl.ANY)
HBM = pl.BlockSpec(memory_space=pltpu.HBM)


def params(mib):
    return pltpu.CompilerParams(vmem_limit_bytes=mib * MIB)


def array(*shape):
    return jax.ShapeDtypeStruct(shape, jnp.bfloat16)


def buffer(*shape):
    return pltpu.VMEM(shape, jnp.bfloat16)


def hbm_array(*shape):
    return pltpu.HBM(shape, jnp.bfloat16)


def in_hbm(*arrays):
    return [pltpu.with_memory_space_constraint(a, pltpu.HBM) for a in arrays]


def cost(flops=1):
    return pl.CostEstimate(flops=flops, bytes_accessed=1, transcendentals=0)


def accumulate(loads, x_ref, w_ref, acc_ref, out_ref, store):
    pieces, count, _ = x_ref.shape
    for i in range(pieces):
        for load in loads[i]:
            load.wait()
        chunk = count if i < pieces - 1 else min(count, LAST_ROWS)
        for start in range(0, count, chunk):
            at = pl.ds(start, chunk)
            term = jnp.dot(x_ref[i, at, :], w_ref[i], preferred_element_type=jnp.float32)
            if i:
                term = acc_ref[at, :] + term
            if i < pieces - 1:
                acc_ref[at, :] = term
            else:
                out_ref[at, :] = term.astype(jnp.bfloat16)
                store(start, chunk)


def load_pieces(x_hbm, x_ref, w_hbms, w_ref, sems):
    pieces, _, size = x_ref.shape
    loads = []
    for i in range(pieces):
        at, left = pl.ds(i * size, size), 0
        loads.append([pltpu.make_async_copy(x_hbm.at[:, at], x_ref.at[i], sems.at[i, 0])])
        for number, w_hbm in enumerate(w_hbms):
            width = w_hbm.shape[1]
            target = w_ref.at[i, :, pl.ds(left, width)]
            loads[-1].append(pltpu.make_async_copy(w_hbm.at[at], target, sems.at[i, 1 + number]))
            left += width
        for load in loads[-1]:
            load.start()
    return loads


def project_kv_kernel(x_hbm, wk_hbm, wv_hbm, kv_hbm, rim_hbm, x_ref, w_ref, acc_ref, kv_ref, in_sems, out_sems):
    loads = load_pieces(x_hbm, x_ref, [wk_hbm, wv_hbm], w_ref, in_sems)
    stores = []

    def store(start, chunk):
        at = pl.ds(start, chunk)
        stores.append(pltpu.make_async_copy(kv_ref.at[at], kv_hbm.at[at], out_sems.at[len(stores)]))
        stores[-1].start()

    accumulate(loads, x_ref, w_ref, acc_ref, kv_ref, store)
    last = pl.ds(kv_ref.shape[0] - WINDOW, WINDOW)
    stores.append(pltpu.make_async_copy(kv_ref.at[last], rim_hbm, out_sems.at[len(stores)]))
    stores[-1].start()
    for copy in stores:
        copy.wait()


def project_kv(rows, w_key, w_value):
    count, depth = rows.shape
    width = w_key.shape[1]
    return pl.pallas_call(
        project_kv_kernel,
        out_shape=[hbm_array(count, 2 * width), hbm_array(WINDOW, 2 * width)],
        in_specs=[HBM] * 3,
        out_specs=[HBM] * 2,
        scratch_shapes=[
            buffer(PIECES, count, depth // PIECES),
            buffer(PIECES, depth // PIECES, 2 * width),
            pltpu.VMEM((count, 2 * width), jnp.float32),
            buffer(count, 2 * width),
            pltpu.SemaphoreType.DMA((PIECES, 3)),
            pltpu.SemaphoreType.DMA((1 + -(-count // min(count, LAST_ROWS)),)),
        ],
        compiler_params=params(16),
        cost_estimate=cost(),
    )(*in_hbm(rows, w_key, w_value))


def project_q_kernel(part, x_hbm, w_hbm, q_ref, *refs):
    part_hbms, (x_ref, w_ref, acc_ref, in_sems, out_sems) = refs[:-5], refs[-5:]
    loads = load_pieces(x_hbm, x_ref, [w_hbm], w_ref, in_sems)
    stores = []

    def store(start, chunk):
        for index in range(len(part_hbms)):
            if start < (index + 1) * part <= start + chunk:
                source = q_ref.at[pl.ds(index * part, part)]
                stores.append(pltpu.make_async_copy(source, part_hbms[index], out_sems.at[index]))
                stores[-1].start()

    accumulate(loads, x_ref, w_ref, acc_ref, q_ref, store)
    for copy in stores:
        copy.wait()


def project_q(rows, weight, parts):
    count, depth = rows.shape
    width = weight.shape[1]
    part = count // parts
    return pl.pallas_call(
        functools.partial(project_q_kernel, part),
        out_shape=[array(count, width)] + [hbm_array(part, width)] * (parts - 1),
        in_specs=[HBM] * 2,
        out_specs=[VMEM] + [HBM] * (parts - 1),
        scratch_shapes=[
            buffer(PIECES, count, depth // PIECES),
            buffer(PIECES, depth // PIECES, width),
            pltpu.VMEM((count, width), jnp.float32),
            pltpu.SemaphoreType.DMA((PIECES, 2)),
            pltpu.SemaphoreType.DMA((parts - 1,)),
        ],
        compiler_params=params(20),
        cost_estimate=cost(),
    )(*in_hbm(rows, weight))


def nothing_kernel(*refs):
    pass


def once(block, arrays):
    return pl.pallas_call(
        nothing_kernel,
        out_shape=hbm_array(*block.shape),
        in_specs=[HBM] + [ANY] * len(arrays),
        out_specs=HBM,
        input_output_aliases={0: 0},
        cost_estimate=cost(),
    )(*in_hbm(block), *arrays)


def choose_kernel(which_ref, a_hbm, b_hbm, *refs):
    out_ref, sem = refs[-2:]
    for flag, source in ((1, a_hbm), (0, b_hbm)):

        @pl.when(which_ref[0] == flag)
        def _(source=source):
            pltpu.make_async_copy(source, out_ref, sem).start()

    pltpu.make_async_copy(b_hbm, out_ref, sem).wait()


def choose(which, a, b, after):
    return pl.pallas_call(
        choose_kernel,
        out_shape=array(*a.shape),
        in_specs=[SMEM] + [HBM] * 2 + [ANY] * len(after),
        out_specs=VMEM,
        scratch_shapes=[pltpu.SemaphoreType.DMA],
        compiler_params=params(16),
        cost_estimate=cost(),
    )(which, *in_hbm(a, b), *after)


def band_kernel(blocks_of, first_ref, q_ref, kv_ref, *refs):
    rim_ref, (out_hbm, token_ref, out_ref, sems) = refs[0], refs[-4:]
    token_ref[...] = jnp.zeros_like(token_ref)
    width = kv_ref.shape[1] // 2
    first = first_ref[0] == 1
    row = lax.broadcasted_iota(jnp.int32, (GROUP * BAND, BAND), 0) % BAND
    column = lax.broadcasted_iota(jnp.int32, (GROUP * BAND, BAND), 1)
    behind = column >= row
    ahead = column <= row
    ones = jnp.ones((BAND, HD), jnp.bfloat16)

    def chunk(index, low, high):
        if index < 0:
            return rim_ref[pl.ds(WINDOW + index * BAND, BAND), low:high]
        return kv_ref[pl.ds(index * BAND, BAND), low:high]

    blocks = WINDOW // BAND + 1
    stores = []
    for number, index in enumerate(blocks_of):
        for c in range(HK):
            q = jnp.concatenate(
                [q_ref[pl.ds(index * BAND, BAND), h * HD : (h + 1) * HD] for h in range(c * GROUP, (c + 1) * GROUP)],
                axis=0,
            )
            at = [index + j - (blocks - 1) for j in range(blocks)]
            k = jnp.concatenate([chunk(a, c * HD, (c + 1) * HD) for a in at], axis=0)
            v = jnp.concatenate([chunk(a, width + c * HD, width + (c + 1) * HD) for a in at], axis=0)
            v = jnp.concatenate([v, jnp.concatenate([ones] * blocks, axis=0)], axis=1)
            s = lax.dot_general(q, k, (((1,), (1,)), ((), ())), preferred_element_type=jnp.float32)
            tiles = []
            for j in range(blocks):
                t = s[:, j * BAND : (j + 1) * BAND]
                allowed = None
                if j == 0:
                    allowed = behind
                elif j == blocks - 1:
                    allowed = ahead
                if at[j] < 0:
                    some = jnp.logical_not(first)
                    allowed = some if allowed is None else jnp.logical_and(allowed, some)
                if allowed is not None:
                    t = jnp.where(allowed, t, -jnp.inf)
                tiles.append(t)
            top = functools.reduce(jnp.maximum, tiles)
            top = jnp.max(top, axis=-1, keepdims=True)
            p = jnp.concatenate(
                [jnp.exp2((t - top) * (SCALE * math.log2(math.e))).astype(jnp.bfloat16) for t in tiles], axis=1
            )
            o = jnp.dot(p, v, preferred_element_type=jnp.float32)
            o = (o[:, :HD] / o[:, HD:]).astype(jnp.bfloat16)
            for g in range(GROUP):
                h = c * GROUP + g
                out_ref[pl.ds(number * BAND, BAND), h * HD : (h + 1) * HD] = o[g * BAND : (g + 1) * BAND]
        stores.append(
            pltpu.make_async_copy(
                out_ref.at[pl.ds(number * BAND, BAND)], out_hbm.at[pl.ds(index * BAND, BAND)], sems.at[number]
            )
        )
        stores[-1].start()
    for store in stores:
        store.wait()


def band_attend(first, query, kv, rim, blocks_of, out, after, flops=1):
    count, width = query.shape
    rows = len(blocks_of) * BAND
    inside = [rim] if blocks_of[0] * BAND < WINDOW else []
    given = [] if out is None else [out]
    return pl.pallas_call(
        functools.partial(band_kernel, blocks_of),
        out_shape=[array(count, width), array(16, HD)],
        in_specs=[SMEM] + [VMEM] * (2 + len(inside)) + [ANY] * len(given + after),
        out_specs=[ANY, VMEM],
        scratch_shapes=[buffer(rows, width), pltpu.SemaphoreType.DMA((len(blocks_of),))],
        input_output_aliases={3 + len(inside): 0} if given else {},
        compiler_params=params(16),
        cost_estimate=cost(flops),
    )(first, query, kv, *inside, *given, *after)


def depth_kernel(cases, which_ref, *refs):
    q_hbms, (kv_hbm, out_hbm, q_ref, kv_ref, out_ref, sems) = refs[:cases], refs[cases:]
    steps, count, width = kv_ref.shape
    width //= 2
    chunk = min(count, 32)
    chunks = [pl.ds(start, chunk) for start in range(0, count, chunk)]
    last = pl.ds(q_hbms[0].shape[0] - count, count)
    loads = []
    for case, source in enumerate([q_hbms[0].at[last], *q_hbms[1:]]):

        @pl.when(which_ref[0] == case)
        def _(source=source):
            pltpu.make_async_copy(source, q_ref, sems.at[0]).start()

    for i, rows in enumerate(chunks):
        loads.append(pltpu.make_async_copy(kv_hbm.at[:, rows], kv_ref.at[:, rows], sems.at[1 + i]))
        loads[-1].start()
    pltpu.make_async_copy(q_hbms[1], q_ref, sems.at[0]).wait()
    stores = []
    for i, rows in enumerate(chunks):
        loads[i].wait()
        for c in range(HK):
            keys = [kv_ref[s, rows, c * HD : (c + 1) * HD].astype(jnp.float32) for s in range(steps)]
            values = [
                kv_ref[s, rows, width + c * HD : width + (c + 1) * HD].astype(jnp.float32) for s in range(steps)
            ]
            for h in range(c * GROUP, (c + 1) * GROUP):
                q = q_ref[rows, h * HD : (h + 1) * HD].astype(jnp.float32) * (SCALE * math.log2(math.e))
                scores = [jnp.sum(q * k, axis=-1, keepdims=True) for k in keys]
                top = functools.reduce(jnp.maximum, scores)
                expo = [jnp.exp2(s - top) for s in scores]
                part = 1.0 / functools.reduce(jnp.add, expo)
                out = functools.reduce(jnp.add, [(e * part) * v for e, v in zip(expo, values)])
                out_ref[rows, h * HD : (h + 1) * HD] = out.astype(jnp.bfloat16)
        stores.append(pltpu.make_async_copy(out_ref.at[rows], out_hbm.at[rows], sems.at[1 + len(chunks) + i]))
        stores[-1].start()
    for store in stores:
        store.wait()


def depth_attend(which, query, queries, kv):
    steps, count, _ = kv.shape
    shape = (count, query.shape[1])
    return pl.pallas_call(
        functools.partial(depth_kernel, 1 + len(queries)),
        out_shape=array(*shape),
        in_specs=[SMEM, ANY] + [HBM] * len(queries) + [HBM],
        out_specs=ANY,
        scratch_shapes=[
            buffer(*shape),
            buffer(*kv.shape),
            buffer(*shape),
            pltpu.SemaphoreType.DMA((1 + 2 * -(-count // min(count, 32)),)),
        ],
        compiler_params=params(16),
        cost_estimate=cost(),
    )(which, query, *in_hbm(*queries, kv))


def flag(value):
    return value.astype(jnp.int32).reshape(1)


def body(states, w_query, w_key, w_value):
    local = states[0]
    rows = local.shape[0]
    steps = lax.axis_size("depth")
    here = lax.axis_index("depth")
    part = rows // steps
    shards = lax.axis_size("tok")
    root, buddy = steps - 1, steps - 2
    shard = lax.axis_index("tok")
    first, is_root, both = flag(shard == 0), flag(here == root), range(2)
    even = list(range(0, buddy, 2))
    by_buddy, split = even[:RELAYS], even[RELAYS : RELAYS + 1]
    straight = [i for i in range(buddy) if i // 2 * 2 not in by_buddy and i not in split]

    def send(block, *moves):
        pairs = [tuple(step * shards + t for step in pair) for t in range(shards) for pair in moves[t % len(moves)]]
        return lax.ppermute(block, ("depth", "tok"), pairs)

    kv, rim = project_kv(local, w_key, w_value)
    spread = lax.all_to_all(kv.reshape(steps, part, kv.shape[1]), "depth", split_axis=0, concat_axis=0, tiled=True)
    rim = lax.ppermute(rim, "tok", [(t, (t + 1) % shards) for t in range(shards)])
    query, *queries = project_q(local, w_query, steps)

    relayed = [send(queries[index], [(root, buddy)]) for index in by_buddy]
    halved = [send(queries[index], [(root, buddy)], [(root, index)]) for index in split]
    direct = [send(queries[index], [(root, index)]) for index in straight]
    cases = direct + halved
    owners = [[(i, p) for p in both] for i in straight] + [[(i, 1)] for i in split]
    blocks = list(range(rows // BAND))
    high = len(blocks) * BAND_LAST // 8
    window_out, token = band_attend(first, query, kv, rim, blocks[high:], None, [])
    beside = []
    for index, got in zip(by_buddy, relayed):
        waits = [token] + (direct if index == by_buddy[-1] else [])
        block = choose(is_root, queries[index + 1], got, waits)
        first_block = block if not beside else first_block
        beside.append(send(block, [(buddy, index), (root, index + 1)]))
        owners.append([(i, p) for i in (index, index + 1) for p in both])
    own = once(queries[buddy], [first_block])
    cases += beside + [send(own, [(root, buddy)])]
    owners.append([(buddy, p) for p in both])
    for index, half in zip(split, halved):
        cases.append(send(half, [(buddy, index)], []))
        owners.append([(index, 0)])
    window_out, _ = band_attend(first, query, kv, rim, blocks[:high], window_out, beside[:-1], LAST_FLOPS)
    which = sum(
        (jnp.where((here == i) & (shard % 2 == p), case + 1, 0) for case, ends in enumerate(owners) for i, p in ends), 0
    )
    depth_out = depth_attend(flag(which), query, cases, spread)
    return (window_out[None], depth_out)


def solution(mesh):
    in_specs = (P("depth", "tok", None), P(), P(), P())
    out_specs = (P("depth", "tok", None), P(("tok", "depth"), None))
    return jax.shard_map(body, mesh=mesh, in_specs=in_specs, out_specs=out_specs, check_vma=False)
```

```python
import functools
import math

import jax
import jax.numpy as jnp
from jax import lax
from jax.experimental import pallas as pl
from jax.experimental.pallas import tpu as pltpu
from jax.sharding import PartitionSpec as P

HQ = 8
HK = 2
HD = 128
WINDOW = 256
GROUP = HQ // HK
SCALE = 1.0 / math.sqrt(HD)
BAND = 128
RELAYS = 2
LAST_FLOPS = 10**9
PIECES = 4
BAND_LAST = 3
LAST_ROWS = 256
MIB = 1024 * 1024
VMEM = pl.BlockSpec(memory_space=pltpu.VMEM)
SMEM = pl.BlockSpec(memory_space=pltpu.SMEM)
ANY = pl.BlockSpec(memory_space=pl.ANY)
HBM = pl.BlockSpec(memory_space=pltpu.HBM)


def params(mib):
    return pltpu.CompilerParams(vmem_limit_bytes=mib * MIB)


def array(*shape):
    return jax.ShapeDtypeStruct(shape, jnp.bfloat16)


def buffer(*shape):
    return pltpu.VMEM(shape, jnp.bfloat16)


def hbm_array(*shape):
    return pltpu.HBM(shape, jnp.bfloat16)


def in_hbm(*arrays):
    return [pltpu.with_memory_space_constraint(a, pltpu.HBM) for a in arrays]


def cost(flops=1):
    return pl.CostEstimate(flops=flops, bytes_accessed=1, transcendentals=0)


def accumulate(loads, x_ref, w_ref, acc_ref, out_ref, store):
    pieces, count, _ = x_ref.shape
    for i in range(pieces):
        for load in loads[i]:
            load.wait()
        chunk = count if i < pieces - 1 else min(count, LAST_ROWS)
        for start in range(0, count, chunk):
            at = pl.ds(start, chunk)
            term = jnp.dot(x_ref[i, at, :], w_ref[i], preferred_element_type=jnp.float32)
            if i:
                term = acc_ref[at, :] + term
            if i < pieces - 1:
                acc_ref[at, :] = term
            else:
                out_ref[at, :] = term.astype(jnp.bfloat16)
                store(start, chunk)


def load_pieces(x_hbm, x_ref, w_hbms, w_ref, sems):
    pieces, _, size = x_ref.shape
    loads = []
    for i in range(pieces):
        at, left = pl.ds(i * size, size), 0
        loads.append([pltpu.make_async_copy(x_hbm.at[:, at], x_ref.at[i], sems.at[i, 0])])
        for number, w_hbm in enumerate(w_hbms):
            width = w_hbm.shape[1]
            target = w_ref.at[i, :, pl.ds(left, width)]
            loads[-1].append(pltpu.make_async_copy(w_hbm.at[at], target, sems.at[i, 1 + number]))
            left += width
        for load in loads[-1]:
            load.start()
    return loads


def project_kv_kernel(x_hbm, wk_hbm, wv_hbm, kv_hbm, rim_hbm, x_ref, w_ref, acc_ref, kv_ref, in_sems, out_sems):
    loads = load_pieces(x_hbm, x_ref, [wk_hbm, wv_hbm], w_ref, in_sems)
    stores = []

    def store(start, chunk):
        at = pl.ds(start, chunk)
        stores.append(pltpu.make_async_copy(kv_ref.at[at], kv_hbm.at[at], out_sems.at[len(stores)]))
        stores[-1].start()

    accumulate(loads, x_ref, w_ref, acc_ref, kv_ref, store)
    last = pl.ds(kv_ref.shape[0] - WINDOW, WINDOW)
    stores.append(pltpu.make_async_copy(kv_ref.at[last], rim_hbm, out_sems.at[len(stores)]))
    stores[-1].start()
    for copy in stores:
        copy.wait()


def project_kv(rows, w_key, w_value):
    count, depth = rows.shape
    width = w_key.shape[1]
    return pl.pallas_call(
        project_kv_kernel,
        out_shape=[hbm_array(count, 2 * width), hbm_array(WINDOW, 2 * width)],
        in_specs=[HBM] * 3,
        out_specs=[HBM] * 2,
        scratch_shapes=[
            buffer(PIECES, count, depth // PIECES),
            buffer(PIECES, depth // PIECES, 2 * width),
            pltpu.VMEM((count, 2 * width), jnp.float32),
            buffer(count, 2 * width),
            pltpu.SemaphoreType.DMA((PIECES, 3)),
            pltpu.SemaphoreType.DMA((1 + -(-count // min(count, LAST_ROWS)),)),
        ],
        compiler_params=params(16),
        cost_estimate=cost(),
    )(*in_hbm(rows, w_key, w_value))


def project_q_kernel(part, x_hbm, w_hbm, q_ref, *refs):
    part_hbms, (x_ref, w_ref, acc_ref, in_sems, out_sems) = refs[:-5], refs[-5:]
    loads = load_pieces(x_hbm, x_ref, [w_hbm], w_ref, in_sems)
    stores = []

    def store(start, chunk):
        for index in range(len(part_hbms)):
            if start < (index + 1) * part <= start + chunk:
                source = q_ref.at[pl.ds(index * part, part)]
                stores.append(pltpu.make_async_copy(source, part_hbms[index], out_sems.at[index]))
                stores[-1].start()

    accumulate(loads, x_ref, w_ref, acc_ref, q_ref, store)
    for copy in stores:
        copy.wait()


def project_q(rows, weight, parts):
    count, depth = rows.shape
    width = weight.shape[1]
    part = count // parts
    return pl.pallas_call(
        functools.partial(project_q_kernel, part),
        out_shape=[array(count, width)] + [hbm_array(part, width)] * (parts - 1),
        in_specs=[HBM] * 2,
        out_specs=[VMEM] + [HBM] * (parts - 1),
        scratch_shapes=[
            buffer(PIECES, count, depth // PIECES),
            buffer(PIECES, depth // PIECES, width),
            pltpu.VMEM((count, width), jnp.float32),
            pltpu.SemaphoreType.DMA((PIECES, 2)),
            pltpu.SemaphoreType.DMA((parts - 1,)),
        ],
        compiler_params=params(20),
        cost_estimate=cost(),
    )(*in_hbm(rows, weight))


def nothing_kernel(*refs):
    pass


def once(block, arrays):
    return pl.pallas_call(
        nothing_kernel,
        out_shape=hbm_array(*block.shape),
        in_specs=[HBM] + [ANY] * len(arrays),
        out_specs=HBM,
        input_output_aliases={0: 0},
        cost_estimate=cost(),
    )(*in_hbm(block), *arrays)


def choose_kernel(which_ref, a_hbm, b_hbm, *refs):
    out_ref, sem = refs[-2:]
    for flag, source in ((1, a_hbm), (0, b_hbm)):

        @pl.when(which_ref[0] == flag)
        def _(source=source):
            pltpu.make_async_copy(source, out_ref, sem).start()

    pltpu.make_async_copy(b_hbm, out_ref, sem).wait()


def nothing_kernel(*refs):
    pass


def once(block, arrays):
    return pl.pallas_call(
        nothing_kernel,
        out_shape=hbm_array(*block.shape),
        in_specs=[HBM] + [ANY] * len(arrays),
        out_specs=HBM,
        input_output_aliases={0: 0},
        cost_estimate=cost(),
    )(*in_hbm(block), *arrays)


def choose_kernel(which_ref, a_hbm, b_hbm, *refs):
    out_ref, sem = refs[-2:]
    for flag, source in ((1, a_hbm), (0, b_hbm)):

        @pl.when(which_ref[0] == flag)
        def _(source=source):
            pltpu.make_async_copy(source, out_ref, sem).start()

    pltpu.make_async_copy(b_hbm, out_ref, sem).wait()


def choose(which, a, b, after):
    return pl.pallas_call(
        choose_kernel,
        out_shape=buffer(*a.shape),
        in_specs=[SMEM, HBM] + [ANY] * (1 + len(after)),
        out_specs=VMEM,
        scratch_shapes=[pltpu.SemaphoreType.DMA],
        compiler_params=params(16),
        cost_estimate=cost(),
    )(which, *in_hbm(a), b, *after)


def band_kernel(blocks_of, first_ref, q_ref, kv_ref, *refs):
    rim_ref, (out_hbm, token_ref, out_ref, sems) = refs[0], refs[-4:]
    token_ref[...] = jnp.zeros_like(token_ref)
    width = kv_ref.shape[1] // 2
    first = first_ref[0] == 1
    row = lax.broadcasted_iota(jnp.int32, (GROUP * BAND, BAND), 0) % BAND
    column = lax.broadcasted_iota(jnp.int32, (GROUP * BAND, BAND), 1)
    behind = column >= row
    ahead = column <= row
    ones = jnp.ones((BAND, HD), jnp.bfloat16)

    def chunk(index, low, high):
        if index < 0:
            return rim_ref[pl.ds(WINDOW + index * BAND, BAND), low:high]
        return kv_ref[pl.ds(index * BAND, BAND), low:high]

    blocks = WINDOW // BAND + 1
    stores = []
    for number, index in enumerate(blocks_of):
        for c in range(HK):
            q = jnp.concatenate(
                [q_ref[pl.ds(index * BAND, BAND), h * HD : (h + 1) * HD] for h in range(c * GROUP, (c + 1) * GROUP)],
                axis=0,
            )
            at = [index + j - (blocks - 1) for j in range(blocks)]
            k = jnp.concatenate([chunk(a, c * HD, (c + 1) * HD) for a in at], axis=0)
            v = jnp.concatenate([chunk(a, width + c * HD, width + (c + 1) * HD) for a in at], axis=0)
            v = jnp.concatenate([v, jnp.concatenate([ones] * blocks, axis=0)], axis=1)
            s = lax.dot_general(q, k, (((1,), (1,)), ((), ())), preferred_element_type=jnp.float32)
            tiles = []
            for j in range(blocks):
                t = s[:, j * BAND : (j + 1) * BAND]
                allowed = None
                if j == 0:
                    allowed = behind
                elif j == blocks - 1:
                    allowed = ahead
                if at[j] < 0:
                    some = jnp.logical_not(first)
                    allowed = some if allowed is None else jnp.logical_and(allowed, some)
                if allowed is not None:
                    t = jnp.where(allowed, t, -jnp.inf)
                tiles.append(t)
            top = functools.reduce(jnp.maximum, tiles)
            top = jnp.max(top, axis=-1, keepdims=True)
            p = jnp.concatenate(
                [jnp.exp2((t - top) * (SCALE * math.log2(math.e))).astype(jnp.bfloat16) for t in tiles], axis=1
            )
            o = jnp.dot(p, v, preferred_element_type=jnp.float32)
            o = (o[:, :HD] / o[:, HD:]).astype(jnp.bfloat16)
            for g in range(GROUP):
                h = c * GROUP + g
                out_ref[pl.ds(number * BAND, BAND), h * HD : (h + 1) * HD] = o[g * BAND : (g + 1) * BAND]
        stores.append(
            pltpu.make_async_copy(
                out_ref.at[pl.ds(number * BAND, BAND)], out_hbm.at[pl.ds(index * BAND, BAND)], sems.at[number]
            )
        )
        stores[-1].start()
    for store in stores:
        store.wait()


def band_attend(first, query, kv, rim, blocks_of, out, after, flops=1):
    count, width = query.shape
    rows = len(blocks_of) * BAND
    inside = [rim] if blocks_of[0] * BAND < WINDOW else []
    given = [] if out is None else [out]
    return pl.pallas_call(
        functools.partial(band_kernel, blocks_of),
        out_shape=[array(count, width), array(16, HD)],
        in_specs=[SMEM] + [VMEM] * (2 + len(inside)) + [ANY] * len(given + after),
        out_specs=[ANY, VMEM],
        scratch_shapes=[buffer(rows, width), pltpu.SemaphoreType.DMA((len(blocks_of),))],
        input_output_aliases={3 + len(inside): 0} if given else {},
        compiler_params=params(10),
        cost_estimate=cost(flops),
    )(first, query, kv, *inside, *given, *after)


def depth_kernel(cases, which_ref, *refs):
    q_hbms, (kv_hbm, out_hbm, q_ref, kv_ref, out_ref, sems) = refs[:cases], refs[cases:]
    steps, count, width = kv_ref.shape
    width //= 2
    chunk = min(count, 64)
    chunks = [pl.ds(start, chunk) for start in range(0, count, chunk)]
    last = pl.ds(q_hbms[0].shape[0] - count, count)
    loads = []
    for case, source in enumerate([q_hbms[0].at[last], *q_hbms[1:]]):

        @pl.when(which_ref[0] == case)
        def _(source=source):
            pltpu.make_async_copy(source, q_ref, sems.at[0]).start()

    for i, rows in enumerate(chunks):
        loads.append(pltpu.make_async_copy(kv_hbm.at[:, rows], kv_ref.at[:, rows], sems.at[1 + i]))
        loads[-1].start()
    pltpu.make_async_copy(q_hbms[1], q_ref, sems.at[0]).wait()
    stores = []
    for i, rows in enumerate(chunks):
        loads[i].wait()
        for c in range(HK):
            keys = [kv_ref[s, rows, c * HD : (c + 1) * HD].astype(jnp.float32) for s in range(steps)]
            values = [
                kv_ref[s, rows, width + c * HD : width + (c + 1) * HD].astype(jnp.float32) for s in range(steps)
            ]
            for h in range(c * GROUP, (c + 1) * GROUP):
                q = q_ref[rows, h * HD : (h + 1) * HD].astype(jnp.float32) * (SCALE * math.log2(math.e))
                scores = [jnp.sum(q * k, axis=-1, keepdims=True) for k in keys]
                top = functools.reduce(jnp.maximum, scores)
                expo = [jnp.exp2(s - top) for s in scores]
                part = 1.0 / functools.reduce(jnp.add, expo)
                out = functools.reduce(jnp.add, [(e * part) * v for e, v in zip(expo, values)])
                out_ref[rows, h * HD : (h + 1) * HD] = out.astype(jnp.bfloat16)
        stores.append(pltpu.make_async_copy(out_ref.at[rows], out_hbm.at[rows], sems.at[1 + len(chunks) + i]))
        stores[-1].start()
    for store in stores:
        store.wait()


def depth_attend(which, query, queries, kv):
    steps, count, _ = kv.shape
    shape = (count, query.shape[1])
    return pl.pallas_call(
        functools.partial(depth_kernel, 1 + len(queries)),
        out_shape=array(*shape),
        in_specs=[SMEM, ANY] + [ANY] * len(queries) + [HBM],
        out_specs=ANY,
        scratch_shapes=[
            buffer(*shape),
            buffer(*kv.shape),
            buffer(*shape),
            pltpu.SemaphoreType.DMA((1 + 2 * -(-count // min(count, 64)),)),
        ],
        compiler_params=params(16),
        cost_estimate=cost(),
    )(which, query, *queries, *in_hbm(kv))


def flag(value):
    return value.astype(jnp.int32).reshape(1)


def body(states, w_query, w_key, w_value):
    local = states[0]
    rows = local.shape[0]
    steps = lax.axis_size("depth")
    here = lax.axis_index("depth")
    part = rows // steps
    shards = lax.axis_size("tok")
    root, buddy = steps - 1, steps - 2
    shard = lax.axis_index("tok")
    first, is_root, both = flag(shard == 0), flag(here == root), range(2)
    even = list(range(0, buddy, 2))
    by_buddy, split = even[:RELAYS], even[RELAYS : RELAYS + 1]
    beside_of = {index: index + 1 for index in by_buddy}
    beside_of.update(zip(by_buddy, range(buddy - 1 - 2 * (len(by_buddy) - 1), buddy, 2)))
    straight = [i for i in range(1, buddy, 2) if i not in beside_of.values()] + even[RELAYS + 1 :]

    def send(block, *moves):
        pairs = [tuple(step * shards + t for step in pair) for t in range(shards) for pair in moves[t % len(moves)]]
        return lax.ppermute(block, ("depth", "tok"), pairs)

    kv, rim = project_kv(local, w_key, w_value)
    spread = lax.all_to_all(kv.reshape(steps, part, kv.shape[1]), "depth", split_axis=0, concat_axis=0, tiled=True)
    rim = lax.ppermute(rim, "tok", [(t, (t + 1) % shards) for t in range(shards)])
    query, *queries = project_q(local, w_query, steps)

    relayed = [send(queries[index], [(root, buddy)]) for index in by_buddy]
    halved = [send(queries[index], [(root, buddy)], [(root, index)]) for index in split]
    direct = [send(queries[index], [(root, index)]) for index in straight]
    cases = direct + halved
    owners = [[(i, p) for p in both] for i in straight] + [[(i, 1)] for i in split]
    blocks = list(range(rows // BAND))
    high = len(blocks) * BAND_LAST // 8
    window_out, token = band_attend(first, query, kv, rim, blocks[high:], None, [])
    beside = []
    for index, got in zip(by_buddy, relayed):
        waits = [token] + (direct if index == by_buddy[-1] else [])
        block = choose(is_root, queries[beside_of[index]], got, waits)
        first_block = block if not beside else first_block
        beside.append(send(block, [(buddy, index), (root, beside_of[index])]))
        owners.append([(i, p) for i in (index, beside_of[index]) for p in both])
    own = once(queries[buddy], [first_block])
    cases += beside + [send(own, [(root, buddy)])]
    owners.append([(buddy, p) for p in both])
    for index, half in zip(split, halved):
        cases.append(send(half, [(buddy, index)], []))
        owners.append([(index, 0)])
    window_out, _ = band_attend(first, query, kv, rim, blocks[:high], window_out, beside[:-1], LAST_FLOPS)
    which = sum(
        (jnp.where((here == i) & (shard % 2 == p), case + 1, 0) for case, ends in enumerate(owners) for i, p in ends), 0
    )
    depth_out = depth_attend(flag(which), query, cases, spread)
    return (window_out[None], depth_out)


def solution(mesh):
    in_specs = (P("depth", "tok", None), P(), P(), P())
    out_specs = (P("depth", "tok", None), P(("tok", "depth"), None))
    return jax.shard_map(body, mesh=mesh, in_specs=in_specs, out_specs=out_specs, check_vma=False)
```

```python
import functools
import math

import jax
import jax.numpy as jnp
from jax import lax
from jax.experimental import pallas as pl
from jax.experimental.pallas import tpu as pltpu
from jax.sharding import PartitionSpec as P

HQ = 8
HK = 2
HD = 128
WINDOW = 256
GROUP = HQ // HK
SCALE = 1.0 / math.sqrt(HD)
BAND = 128
RELAYS = 2
LAST_FLOPS = 10**9
PIECES = 4
BAND_LAST = 3
LAST_ROWS = 256
MIB = 1024 * 1024
VMEM = pl.BlockSpec(memory_space=pltpu.VMEM)
SMEM = pl.BlockSpec(memory_space=pltpu.SMEM)
ANY = pl.BlockSpec(memory_space=pl.ANY)
HBM = pl.BlockSpec(memory_space=pltpu.HBM)


def params(mib):
    return pltpu.CompilerParams(vmem_limit_bytes=mib * MIB)


def array(*shape):
    return jax.ShapeDtypeStruct(shape, jnp.bfloat16)


def buffer(*shape):
    return pltpu.VMEM(shape, jnp.bfloat16)


def hbm_array(*shape):
    return pltpu.HBM(shape, jnp.bfloat16)


def in_hbm(*arrays):
    return [pltpu.with_memory_space_constraint(a, pltpu.HBM) for a in arrays]


def cost(flops=1):
    return pl.CostEstimate(flops=flops, bytes_accessed=1, transcendentals=0)


def accumulate(loads, x_ref, w_ref, acc_ref, out_ref, store):
    pieces, count, _ = x_ref.shape
    for i in range(pieces):
        for load in loads[i]:
            load.wait()
        chunk = count if i < pieces - 1 else min(count, LAST_ROWS)
        for start in range(0, count, chunk):
            at = pl.ds(start, chunk)
            term = jnp.dot(x_ref[i, at, :], w_ref[i], preferred_element_type=jnp.float32)
            if i:
                term = acc_ref[at, :] + term
            if i < pieces - 1:
                acc_ref[at, :] = term
            else:
                out_ref[at, :] = term.astype(jnp.bfloat16)
                store(start, chunk)


def load_pieces(x_hbm, x_ref, w_hbms, w_ref, sems):
    pieces, _, size = x_ref.shape
    loads = []
    for i in range(pieces):
        at, left = pl.ds(i * size, size), 0
        loads.append([pltpu.make_async_copy(x_hbm.at[:, at], x_ref.at[i], sems.at[i, 0])])
        for number, w_hbm in enumerate(w_hbms):
            width = w_hbm.shape[1]
            target = w_ref.at[i, :, pl.ds(left, width)]
            loads[-1].append(pltpu.make_async_copy(w_hbm.at[at], target, sems.at[i, 1 + number]))
            left += width
        for load in loads[-1]:
            load.start()
    return loads


def project_kv_kernel(x_hbm, wk_hbm, wv_hbm, kv_hbm, rim_hbm, x_ref, w_ref, acc_ref, kv_ref, in_sems, out_sems):
    loads = load_pieces(x_hbm, x_ref, [wk_hbm, wv_hbm], w_ref, in_sems)
    stores = []

    def store(start, chunk):
        at = pl.ds(start, chunk)
        stores.append(pltpu.make_async_copy(kv_ref.at[at], kv_hbm.at[at], out_sems.at[len(stores)]))
        stores[-1].start()

    accumulate(loads, x_ref, w_ref, acc_ref, kv_ref, store)
    last = pl.ds(kv_ref.shape[0] - WINDOW, WINDOW)
    stores.append(pltpu.make_async_copy(kv_ref.at[last], rim_hbm, out_sems.at[len(stores)]))
    stores[-1].start()
    for copy in stores:
        copy.wait()


def project_kv(rows, w_key, w_value):
    count, depth = rows.shape
    width = w_key.shape[1]
    return pl.pallas_call(
        project_kv_kernel,
        out_shape=[hbm_array(count, 2 * width), hbm_array(WINDOW, 2 * width)],
        in_specs=[HBM] * 3,
        out_specs=[HBM] * 2,
        scratch_shapes=[
            buffer(PIECES, count, depth // PIECES),
            buffer(PIECES, depth // PIECES, 2 * width),
            pltpu.VMEM((count, 2 * width), jnp.float32),
            buffer(count, 2 * width),
            pltpu.SemaphoreType.DMA((PIECES, 3)),
            pltpu.SemaphoreType.DMA((1 + -(-count // min(count, LAST_ROWS)),)),
        ],
        compiler_params=params(16),
        cost_estimate=cost(),
    )(*in_hbm(rows, w_key, w_value))


def project_q_kernel(part, x_hbm, w_hbm, q_ref, *refs):
    part_hbms, (x_ref, w_ref, acc_ref, in_sems, out_sems) = refs[:-5], refs[-5:]
    loads = load_pieces(x_hbm, x_ref, [w_hbm], w_ref, in_sems)
    stores = []

    def store(start, chunk):
        for index in range(len(part_hbms)):
            if start < (index + 1) * part <= start + chunk:
                source = q_ref.at[pl.ds(index * part, part)]
                stores.append(pltpu.make_async_copy(source, part_hbms[index], out_sems.at[index]))
                stores[-1].start()

    accumulate(loads, x_ref, w_ref, acc_ref, q_ref, store)
    for copy in stores:
        copy.wait()


def project_q(rows, weight, parts):
    count, depth = rows.shape
    width = weight.shape[1]
    part = count // parts
    return pl.pallas_call(
        functools.partial(project_q_kernel, part),
        out_shape=[array(count, width)] + [hbm_array(part, width)] * (parts - 1),
        in_specs=[HBM] * 2,
        out_specs=[VMEM] + [HBM] * (parts - 1),
        scratch_shapes=[
            buffer(PIECES, count, depth // PIECES),
            buffer(PIECES, depth // PIECES, width),
            pltpu.VMEM((count, width), jnp.float32),
            pltpu.SemaphoreType.DMA((PIECES, 2)),
            pltpu.SemaphoreType.DMA((parts - 1,)),
        ],
        compiler_params=params(20),
        cost_estimate=cost(),
    )(*in_hbm(rows, weight))


def nothing_kernel(*refs):
    pass


def once(block, arrays):
    return pl.pallas_call(
        nothing_kernel,
        out_shape=hbm_array(*block.shape),
        in_specs=[HBM] + [ANY] * len(arrays),
        out_specs=HBM,
        input_output_aliases={0: 0},
        cost_estimate=cost(),
    )(*in_hbm(block), *arrays)


def choose_kernel(which_ref, a_hbm, b_hbm, *refs):
    out_ref, sem = refs[-2:]
    for flag, source in ((1, a_hbm), (0, b_hbm)):

        @pl.when(which_ref[0] == flag)
        def _(source=source):
            pltpu.make_async_copy(source, out_ref, sem).start()

    pltpu.make_async_copy(b_hbm, out_ref, sem).wait()


def choose(which, a, b, after):
    return pl.pallas_call(
        choose_kernel,
        out_shape=buffer(*a.shape),
        in_specs=[SMEM, HBM] + [ANY] * (1 + len(after)),
        out_specs=VMEM,
        scratch_shapes=[pltpu.SemaphoreType.DMA],
        compiler_params=params(16),
        cost_estimate=cost(),
    )(which, *in_hbm(a), b, *after)


def band_kernel(blocks_of, first_ref, q_ref, kv_ref, *refs):
    rim_ref, (out_hbm, token_ref, out_ref, sems) = refs[0], refs[-4:]
    token_ref[...] = jnp.zeros_like(token_ref)
    width = kv_ref.shape[1] // 2
    first = first_ref[0] == 1
    row = lax.broadcasted_iota(jnp.int32, (GROUP * BAND, BAND), 0) % BAND
    column = lax.broadcasted_iota(jnp.int32, (GROUP * BAND, BAND), 1)
    behind = column >= row
    ahead = column <= row
    ones = jnp.ones((BAND, HD), jnp.bfloat16)

    def chunk(index, low, high):
        if index < 0:
            return rim_ref[pl.ds(WINDOW + index * BAND, BAND), low:high]
        return kv_ref[pl.ds(index * BAND, BAND), low:high]

    blocks = WINDOW // BAND + 1
    stores = []
    for number, index in enumerate(blocks_of):
        for c in range(HK):
            q = jnp.concatenate(
                [q_ref[pl.ds(index * BAND, BAND), h * HD : (h + 1) * HD] for h in range(c * GROUP, (c + 1) * GROUP)],
                axis=0,
            )
            at = [index + j - (blocks - 1) for j in range(blocks)]
            k = jnp.concatenate([chunk(a, c * HD, (c + 1) * HD) for a in at], axis=0)
            v = jnp.concatenate([chunk(a, width + c * HD, width + (c + 1) * HD) for a in at], axis=0)
            v = jnp.concatenate([v, jnp.concatenate([ones] * blocks, axis=0)], axis=1)
            s = lax.dot_general(q, k, (((1,), (1,)), ((), ())), preferred_element_type=jnp.float32)
            tiles = []
            for j in range(blocks):
                t = s[:, j * BAND : (j + 1) * BAND]
                allowed = None
                if j == 0:
                    allowed = behind
                elif j == blocks - 1:
                    allowed = ahead
                if at[j] < 0:
                    some = jnp.logical_not(first)
                    allowed = some if allowed is None else jnp.logical_and(allowed, some)
                if allowed is not None:
                    t = jnp.where(allowed, t, -jnp.inf)
                tiles.append(t)
            top = functools.reduce(jnp.maximum, tiles)
            top = jnp.max(top, axis=-1, keepdims=True)
            p = jnp.concatenate(
                [jnp.exp2((t - top) * (SCALE * math.log2(math.e))).astype(jnp.bfloat16) for t in tiles], axis=1
            )
            o = jnp.dot(p, v, preferred_element_type=jnp.float32)
            o = (o[:, :HD] / o[:, HD:]).astype(jnp.bfloat16)
            for g in range(GROUP):
                h = c * GROUP + g
                out_ref[pl.ds(number * BAND, BAND), h * HD : (h + 1) * HD] = o[g * BAND : (g + 1) * BAND]
        stores.append(
            pltpu.make_async_copy(
                out_ref.at[pl.ds(number * BAND, BAND)], out_hbm.at[pl.ds(index * BAND, BAND)], sems.at[number]
            )
        )
        stores[-1].start()
    for store in stores:
        store.wait()


def band_attend(first, query, kv, rim, blocks_of, out, after, flops=1):
    count, width = query.shape
    rows = len(blocks_of) * BAND
    inside = [rim] if blocks_of[0] * BAND < WINDOW else []
    given = [] if out is None else [out]
    return pl.pallas_call(
        functools.partial(band_kernel, blocks_of),
        out_shape=[array(count, width), array(16, HD)],
        in_specs=[SMEM] + [VMEM] * (2 + len(inside)) + [ANY] * len(given + after),
        out_specs=[ANY, VMEM],
        scratch_shapes=[buffer(rows, width), pltpu.SemaphoreType.DMA((len(blocks_of),))],
        input_output_aliases={3 + len(inside): 0} if given else {},
        compiler_params=params(10),
        cost_estimate=cost(flops),
    )(first, query, kv, *inside, *given, *after)


def depth_kernel(cases, which_ref, *refs):
    q_hbms, (kv_hbm, out_hbm, q_ref, kv_ref, out_ref, sems) = refs[:cases], refs[cases:]
    steps, count, width = kv_ref.shape
    width //= 2
    chunk = min(count, 64)
    chunks = [pl.ds(start, chunk) for start in range(0, count, chunk)]
    last = pl.ds(q_hbms[0].shape[0] - count, count)
    loads = []
    for case, source in enumerate([q_hbms[0].at[last], *q_hbms[1:]]):

        @pl.when(which_ref[0] == case)
        def _(source=source):
            pltpu.make_async_copy(source, q_ref, sems.at[0]).start()

    for i, rows in enumerate(chunks):
        loads.append(pltpu.make_async_copy(kv_hbm.at[:, rows], kv_ref.at[:, rows], sems.at[1 + i]))
        loads[-1].start()
    pltpu.make_async_copy(q_hbms[1], q_ref, sems.at[0]).wait()
    stores = []
    for i, rows in enumerate(chunks):
        loads[i].wait()
        for c in range(HK):
            keys = [kv_ref[s, rows, c * HD : (c + 1) * HD].astype(jnp.float32) for s in range(steps)]
            values = [
                kv_ref[s, rows, width + c * HD : width + (c + 1) * HD].astype(jnp.float32) for s in range(steps)
            ]
            for h in range(c * GROUP, (c + 1) * GROUP):
                q = q_ref[rows, h * HD : (h + 1) * HD].astype(jnp.float32) * (SCALE * math.log2(math.e))
                scores = [jnp.sum(q * k, axis=-1, keepdims=True) for k in keys]
                top = functools.reduce(jnp.maximum, scores)
                expo = [jnp.exp2(s - top) for s in scores]
                part = 1.0 / functools.reduce(jnp.add, expo)
                out = functools.reduce(jnp.add, [(e * part) * v for e, v in zip(expo, values)])
                out_ref[rows, h * HD : (h + 1) * HD] = out.astype(jnp.bfloat16)
        stores.append(pltpu.make_async_copy(out_ref.at[rows], out_hbm.at[rows], sems.at[1 + len(chunks) + i]))
        stores[-1].start()
    for store in stores:
        store.wait()


def depth_attend(which, query, queries, kv):
    steps, count, _ = kv.shape
    shape = (count, query.shape[1])
    return pl.pallas_call(
        functools.partial(depth_kernel, 1 + len(queries)),
        out_shape=array(*shape),
        in_specs=[SMEM, ANY] + [ANY] * len(queries) + [HBM],
        out_specs=ANY,
        scratch_shapes=[
            buffer(*shape),
            buffer(*kv.shape),
            buffer(*shape),
            pltpu.SemaphoreType.DMA((1 + 2 * -(-count // min(count, 64)),)),
        ],
        compiler_params=params(16),
        cost_estimate=cost(),
    )(which, query, *queries, *in_hbm(kv))


def flag(value):
    return value.astype(jnp.int32).reshape(1)


def body(states, w_query, w_key, w_value):
    local = states[0]
    rows = local.shape[0]
    steps = lax.axis_size("depth")
    here = lax.axis_index("depth")
    part = rows // steps
    shards = lax.axis_size("tok")
    root, buddy = steps - 1, steps - 2
    shard = lax.axis_index("tok")
    first, is_root, both = flag(shard == 0), flag(here == root), range(2)
    even = list(range(0, buddy, 2))
    by_buddy, split = even[:RELAYS], even[RELAYS : RELAYS + 1]
    beside_of = {index: index + 1 for index in by_buddy}
    beside_of.update(zip(by_buddy, range(buddy - 1 - 2 * (len(by_buddy) - 1), buddy, 2)))
    straight = [i for i in range(1, buddy, 2) if i not in beside_of.values()] + even[RELAYS + 1 :]

    def send(block, *moves):
        pairs = [tuple(step * shards + t for step in pair) for t in range(shards) for pair in moves[t % len(moves)]]
        return lax.ppermute(block, ("depth", "tok"), pairs)

    kv, rim = project_kv(local, w_key, w_value)
    spread = lax.all_to_all(kv.reshape(steps, part, kv.shape[1]), "depth", split_axis=0, concat_axis=0, tiled=True)
    rim = lax.ppermute(rim, "tok", [(t, (t + 1) % shards) for t in range(shards)])
    query, *queries = project_q(local, w_query, steps)

    relayed = [send(queries[index], [(root, buddy)]) for index in by_buddy]
    halved = [send(queries[index], [(root, buddy)], [(root, index)]) for index in split]
    direct = [send(queries[index], [(root, index)]) for index in straight]
    cases = direct + halved
    owners = [[(i, p) for p in both] for i in straight] + [[(i, 1)] for i in split]
    blocks = list(range(rows // BAND))
    high = len(blocks) * BAND_LAST // 8
    window_out, token = band_attend(first, query, kv, rim, blocks[high:], None, [])
    beside = []
    for index, got in zip(by_buddy, relayed):
        waits = [token] + (direct if index == by_buddy[-1] else [])
        block = choose(is_root, queries[beside_of[index]], got, waits)
        first_block = block if not beside else first_block
        beside.append(send(block, [(buddy, index), (root, beside_of[index])]))
        owners.append([(i, p) for i in (index, beside_of[index]) for p in both])
    own = once(queries[buddy], [first_block])
    cases += beside + [send(own, [(root, buddy)])]
    owners.append([(buddy, p) for p in both])
    for index, half in zip(split, halved):
        cases.append(send(half, [(buddy, index)], []))
        owners.append([(index, 0)])
    window_out, _ = band_attend(first, query, kv, rim, blocks[:high], window_out, beside[:-1], LAST_FLOPS)
    which = sum(
        (jnp.where((here == i) & (shard % 2 == p), case + 1, 0) for case, ends in enumerate(owners) for i, p in ends), 0
    )
    depth_out = depth_attend(flag(which), query, cases, spread)
    return (window_out[None], depth_out)


def solution(mesh):
    in_specs = (P("depth", "tok", None), P(), P(), P())
    out_specs = (P("depth", "tok", None), P(("tok", "depth"), None))
    return jax.shard_map(body, mesh=mesh, in_specs=in_specs, out_specs=out_specs, check_vma=False)
```
